32 devices in a mesh: fsdp: 16 (over z, y, core), tp: 2 (over x).
Axes of the slice: x: 2, y: 2, z: 4, core: 2. Of those that a mesh axis runs over, the one named last changes fastest.
Arguments:
- tokens: bfloat16 [4096, 4096], P('fsdp', 'tp'), may hold values from -6 to 6
- w_feat: bfloat16 [3, 4096, 4096], P(None, 'fsdp', 'tp'), may hold values from -0.09375 to 0.09375
- short_filter: float32 [3, 256, 7], P(None, 'tp'), may hold values from -6 to 6
- long_filter: bfloat16 [256, 128], P('tp'), may hold values from -1.5 to 1.5
- doc_ids: int32 [4096], P('fsdp'), may hold values from 0 to 7, never falling along the last dimension, each value on 1 to 2048 neighbouring positions
- grad_out: bfloat16 [4096, 4096], P('fsdp', 'tp'), may hold values from -6 to 6
Outputs:
- mixed: bfloat16 [4096, 4096], P('fsdp', 'tp')
- input_grad: bfloat16 [4096, 4096], P('fsdp', 'tp')
The draws below stay inside these ranges and needn't reach their ends.
Inputs may be any that keep to these rules, and one draw needn't show every extreme that they name: `doc_ids`: document numbers never fall along the positions; each document covers 1 to 2048 consecutive positions and one covers exactly 2048; every number from 0 to 7 occurs.
All inputs are finite; a program needn't handle non-finite values.
Results may differ from the reference program's by a relative error of at most 0.0081.
Values may be sent and summed in bfloat16 or wider, within the bound.
A program may use at most 192 MiB of HBM per device.

```python
import math
import jax
import jax.numpy as jnp
import numpy as np
from jax import lax

D = 4096
C = 4096
GROUP = 16
TAPS = 128
SHORT = 7
DOC_MOST = 2048
LEN = 4096
DOCS = 8
N_TP = 2


def shard_levels(key, shape, split, low, high):
    def one(position, shards_of):
        steps = jax.random.uniform(jax.random.fold_in(jax.random.fold_in(key, 6), position), (shards_of,), jnp.float32, low / len(split), high / len(split))
        return jnp.repeat(jnp.exp(steps), shape[position] // shards_of).reshape((-1,) + (1,) * (len(shape) - position - 1))

    factor_of = one(*split[0])
    for cut in split[1:]:
        factor_of = factor_of * one(*cut)
    return factor_of


def split_up(count, total, most, lean):
    loads = [(1 << 20) // math.isqrt(rank ** lean) + 1 for rank in range(2, count + 1)]
    spare, counts = total - most - (count - 1), [1] * (count - 1)
    while spare > 0:
        movable = [i for i in range(count - 1) if counts[i] < most]
        whole, left = sum([loads[i] for i in movable]), spare
        for i in movable:
            more = min(most - counts[i], max(1, left * loads[i] // whole), spare)
            counts[i] = counts[i] + more
            spare = spare - more
    return np.array([most] + counts)


def ragged_sizes(stream_key, number_of, total, bound, skew):
    if number_of == 2:
        one = jax.random.randint(stream_key, (), max(1, total - bound), min(bound, total - 1) + 1)
        return jnp.stack([one, total - one])
    lengths = jnp.asarray(split_up(number_of, total, bound, skew), jnp.int32)
    pairs = (number_of - 1) // 2
    source_of, sink = lengths[1:1 + 2 * pairs:2], lengths[2:2 + 2 * pairs:2]
    room = jnp.minimum(source_of - 1, bound - sink)
    moved = jax.random.randint(jax.random.fold_in(stream_key, 1), (pairs,), 0, 1 << 20) % (room + 1)
    lengths = lengths.at[1:1 + 2 * pairs:2].set(source_of - moved).at[2:2 + 2 * pairs:2].set(sink + moved)
    return lengths[jax.random.permutation(jax.random.fold_in(stream_key, 2), number_of)]


def bell_draw(key, dims, spread, reach, cuts=(), kind=jnp.bfloat16):
    result = jax.random.normal(key, dims, jnp.float32) * spread
    if len(cuts) > 0:
        result = shard_levels(key, dims, cuts, -0.22, 0.18) * result
    return jnp.clip(result, min=-reach, max=reach).astype(kind)


def setup_inputs(seed: int = 0) -> dict:
    key_of = jax.random.split(jax.random.key(seed), 7)
    tokens = bell_draw(key_of[0], (LEN, D), 1.0, 6.0, ((0, 16), (1, 2)))
    w_feat = bell_draw(key_of[1], (3, D, C), D ** -0.5, 0.09375, ((1, 16), (2, 2)))
    short_filter = bell_draw(key_of[2], (3, C // GROUP, SHORT), 0.4, 6.0, ((1, 2),), jnp.float32)
    long_filter = bell_draw(key_of[3], (C // GROUP, TAPS), 0.1, 1.5, ((0, 2),))
    doc_ids = jnp.searchsorted(jnp.cumsum(ragged_sizes(key_of[4], DOCS, LEN, DOC_MOST, 1)), jnp.arange(LEN), side="right").astype(jnp.int32)
    grad_out = bell_draw(key_of[5], (LEN, C), 1.0, 6.0, ((0, 16), (1, 2)))
    return dict(tokens=tokens, w_feat=w_feat, short_filter=short_filter, long_filter=long_filter, doc_ids=doc_ids, grad_out=grad_out)


def behind(values, offset, fill):
    length = values.shape[0]
    if offset == 0:
        return values
    padding = jnp.full((offset,) + values.shape[1:], fill, values.dtype)
    return jnp.concatenate([padding, values[:length - offset]], axis=0)


def ahead_of(values, offset, fill):
    if offset == 0:
        return values
    padding = jnp.full((offset,) + values.shape[1:], fill, values.dtype)
    return jnp.concatenate([values[offset:], padding], axis=0)


def long_taps(values, doc_ids, long_full, anti_causal):
    length = values.shape[0]
    width = values.shape[1]
    tap_count = long_full.shape[1]
    zero_rows = jnp.zeros((tap_count, width), jnp.float32)
    fill_docs = jnp.full((tap_count,), -1, jnp.int32)
    if anti_causal:
        padded = jnp.concatenate([values.astype(jnp.float32), zero_rows], axis=0)
        padded_doc = jnp.concatenate([doc_ids, fill_docs], axis=0)
    else:
        padded = jnp.concatenate([zero_rows, values.astype(jnp.float32)], axis=0)
        padded_doc = jnp.concatenate([fill_docs, doc_ids], axis=0)

    def add_tap(tap_id, summed):
        tap_here = jnp.asarray(tap_id).astype(jnp.int32)
        if anti_causal:
            first_row = tap_here
        else:
            first_row = (tap_count - tap_here).astype(jnp.int32)
        shifted = lax.dynamic_slice_in_dim(padded, first_row, length, 0)
        shift_docs = lax.dynamic_slice_in_dim(padded_doc, first_row, length, 0)
        tap_value = lax.dynamic_index_in_dim(long_full, tap_here, 1, False).astype(jnp.float32)
        same_doc = (shift_docs == doc_ids).astype(jnp.float32)
        return summed + tap_value[None, :] * shifted * same_doc[:, None]

    return lax.fori_loop(0, tap_count, add_tap, jnp.zeros((length, width), jnp.float32))


def reference(tokens, w_feat, short_filter, long_filter, doc_ids, grad_out):
    length = tokens.shape[0]
    flat_w = jnp.transpose(w_feat, (1, 0, 2)).reshape(D, 3 * C)
    featured = jnp.dot(tokens, flat_w, preferred_element_type=jnp.float32).astype(jnp.bfloat16).reshape(length, 3, C)
    short_full = jnp.repeat(short_filter, 16, axis=1)
    long_full = jnp.repeat(long_filter, 16, axis=0)
    short_conv = jnp.zeros((length, 3, C), jnp.float32)
    for offset in range(short_filter.shape[2]):
        same_doc = (behind(doc_ids, offset, -1) == doc_ids).astype(jnp.float32)
        short_conv = short_conv + short_full[:, :, offset] * behind(featured, offset, 0).astype(jnp.float32) * same_doc[:, None, None]
    product_kv = (short_conv[:, 1] * short_conv[:, 2]).astype(jnp.bfloat16)
    long_conv = long_taps(product_kv, doc_ids, long_full, False)
    mixed = (short_conv[:, 0] * long_conv).astype(jnp.bfloat16)
    grad_float = grad_out.astype(jnp.float32)
    grad_long = (grad_float * short_conv[:, 0]).astype(jnp.bfloat16)
    grad_query = grad_float * long_conv
    grad_mixed = long_taps(grad_long, doc_ids, long_full, True)
    grad_feat = jnp.stack([grad_query, grad_mixed * short_conv[:, 2], grad_mixed * short_conv[:, 1]], axis=1).astype(jnp.bfloat16)
    grad_sum = jnp.zeros((length, 3, C), jnp.float32)
    for offset in range(short_filter.shape[2]):
        same_doc = (ahead_of(doc_ids, offset, -1) == doc_ids).astype(jnp.float32)
        grad_sum = grad_sum + short_full[:, :, offset] * ahead_of(grad_feat, offset, 0).astype(jnp.float32) * same_doc[:, None, None]
    grad_u = grad_sum.astype(jnp.bfloat16)
    block_width = C // N_TP
    summed = jnp.zeros((length, D), jnp.float32)
    for block_id in range(N_TP):
        grad_block = grad_u[:, :, block_id * block_width:(block_id + 1) * block_width].reshape(length, 3 * block_width)
        weight_block = jnp.transpose(w_feat[:, :, block_id * block_width:(block_id + 1) * block_width], (0, 2, 1)).reshape(3 * block_width, D)
        partial_value = jnp.dot(grad_block, weight_block, preferred_element_type=jnp.float32).astype(jnp.bfloat16)
        summed = summed + partial_value.astype(jnp.float32)
    return mixed, summed.astype(jnp.bfloat16)
```

```python
import functools

import jax
import jax.numpy as jnp
from jax import lax
from jax.experimental import pallas as pl
from jax.experimental.pallas import tpu as pltpu
from jax.sharding import PartitionSpec as P

LANES = 128
EDGE = 16


def shifted(value, axis, steps):
    count = lax.axis_size(axis)
    first, last = max(0, -steps), min(count, count - steps)
    return lax.ppermute(value, axis, [(at, at + steps) for at in range(first, last)])


def rotated(value, axis, steps):
    count = lax.axis_size(axis)
    return lax.ppermute(value, axis, [(at, (at + steps) % count) for at in range(count)])


def gather_columns(value, axis):
    count = lax.axis_size(axis)
    width = value.shape[1]
    here = lax.axis_index(axis)
    whole = jnp.zeros((value.shape[0], width * count), value.dtype)
    for step in range(count):
        block = value if step == 0 else rotated(value, axis, step)
        owner = (here - step) % count
        whole = lax.dynamic_update_slice(whole, block, (0, owner * width))
    return whole


def toeplitz(long_filter, anti_causal):
    taps = long_filter.shape[1]
    row = lax.broadcasted_iota(jnp.int32, (taps, 2 * taps), 0)
    column = lax.broadcasted_iota(jnp.int32, (taps, 2 * taps), 1)
    lag = column - row if anti_causal else row + taps - column
    tap = lax.broadcasted_iota(jnp.int32, (taps, taps, 2 * taps), 0)
    one_hot = (tap == lag[None]).astype(long_filter.dtype).reshape(taps, 2 * taps * taps)
    table = jnp.dot(long_filter, one_hot, preferred_element_type=jnp.float32)
    return table.astype(long_filter.dtype).reshape(long_filter.shape[0], taps, 2 * taps)


def conv_kernel(
    rows, taps, short,
    u_q, u_kv, grad, filters, t_fwd, t_bwd, m_fwd, m_bwd, back, ahead,
    mixed, grad_u,
    f32_u, conv, prod, glong, feat,
):
    near = rows + EDGE
    far = rows + taps + EDGE
    groups = t_fwd.shape[0]
    lane_group = lax.broadcasted_iota(jnp.int32, (1, LANES), 1) // (LANES // groups)

    def short_conv(role, source, first):
        f32_u[...] = source.astype(jnp.float32)
        total = filters[role, 0:1, :] * f32_u[pl.ds(EDGE, far), :]
        for i in range(1, short):
            term = filters[role, i : i + 1, :] * f32_u[pl.ds(EDGE - i, far), :]
            total = total + jnp.where(back[pl.ds(first, far), :] >= i, term, 0.0)
        return total

    conv[0] = short_conv(0, u_q[...], taps)
    conv[1] = short_conv(1, u_kv[0], 0)
    conv[2] = short_conv(2, u_kv[1], 0)
    pad = jnp.zeros((prod.shape[0] - far, LANES), prod.dtype)
    prod[pl.ds(0, far), :] = (conv[1] * conv[2]).astype(prod.dtype)
    prod[pl.ds(far, pad.shape[0]), :] = pad
    glong[pl.ds(0, far), :] = (grad[...].astype(jnp.float32) * conv[0]).astype(glong.dtype)
    glong[pl.ds(far, pad.shape[0]), :] = pad

    def long_conv(table, masks, source, start):
        count = min(taps, near - start)
        kernel = table[:, pl.ds(0, count), :] * masks[pl.ds(start, count), :][None]
        out = jnp.dot(
            kernel.reshape(groups * count, 2 * taps),
            source[pl.ds(start, 2 * taps), :],
            preferred_element_type=jnp.float32,
        ).reshape(groups, count, LANES)
        total = jnp.where(lane_group == 0, out[0], 0.0)
        for g in range(1, groups):
            total = jnp.where(lane_group == g, out[g], total)
        return total

    def rounded(value):
        return value.astype(jnp.bfloat16).astype(jnp.float32)

    for start in range(0, near, taps):
        count = min(taps, near - start)
        here = pl.ds(start, count)
        behind = pl.ds(start + taps, count)
        lc = long_conv(t_fwd, m_fwd, prod, start)
        gm = long_conv(t_bwd, m_bwd, glong, start)
        if start < rows:
            mixed[here, :] = (conv[0, here, :] * lc).astype(mixed.dtype)
        feat[0, here, :] = rounded(grad[here, :].astype(jnp.float32) * lc)
        feat[1, here, :] = rounded(gm * conv[2, behind, :])
        feat[2, here, :] = rounded(gm * conv[1, behind, :])
    for role in range(3):
        total = filters[role, 0:1, :] * feat[role, pl.ds(0, rows), :]
        for i in range(1, short):
            term = filters[role, i : i + 1, :] * feat[role, pl.ds(i, rows), :]
            total = total + jnp.where(ahead[...] >= i, term, 0.0)
        grad_u[role] = total.astype(grad_u.dtype)


def convolve(rows, taps, short, first, u_q, u_kv, grad, filters, t_fwd, t_bwd, m_fwd, m_bwd, back, ahead):
    width = u_q.shape[1]
    wide = u_q.shape[0]
    near, far = rows + EDGE, rows + taps + EDGE
    groups = t_fwd.shape[0] * LANES // grad.shape[1]
    first = first // LANES
    padded = rows + 2 * taps
    whole = lambda *shape: pl.BlockSpec(shape, lambda n: (0,) * len(shape))
    return pl.pallas_call(
        functools.partial(conv_kernel, rows, taps, short),
        grid=(width // LANES,),
        in_specs=[
            pl.BlockSpec((wide, LANES), lambda n: (0, n)),
            pl.BlockSpec((2, wide, LANES), lambda n: (0, 0, n)),
            pl.BlockSpec((far, LANES), lambda n: (0, n + first)),
            pl.BlockSpec((3, 8, LANES), lambda n: (0, 0, n + first)),
            pl.BlockSpec((groups, taps, 2 * taps), lambda n: (n + first, 0, 0)),
            pl.BlockSpec((groups, taps, 2 * taps), lambda n: (n + first, 0, 0)),
            whole(near, 2 * taps),
            whole(near, 2 * taps),
            whole(*back.shape),
            whole(*ahead.shape),
        ],
        out_specs=[
            pl.BlockSpec((rows, LANES), lambda n: (0, n)),
            pl.BlockSpec((3, rows, LANES), lambda n: (0, 0, n)),
        ],
        out_shape=[
            jax.ShapeDtypeStruct((rows, width), jnp.bfloat16),
            jax.ShapeDtypeStruct((3, rows, width), jnp.bfloat16),
        ],
        scratch_shapes=[
            pltpu.VMEM((wide, LANES), jnp.float32),
            pltpu.VMEM((3, far, LANES), jnp.float32),
            pltpu.VMEM((padded, LANES), jnp.bfloat16),
            pltpu.VMEM((padded, LANES), jnp.bfloat16),
            pltpu.VMEM((3, near, LANES), jnp.float32),
        ],
        compiler_params=pltpu.CompilerParams(vmem_limit_bytes=24 * 1024 * 1024),
        cost_estimate=pl.CostEstimate(
            flops=width * rows * taps * 64, bytes_accessed=width * rows * 40, transcendentals=0
        ),
    )(u_q, u_kv, grad, filters, t_fwd, t_bwd, m_fwd, m_bwd, back, ahead)


def chunk_sizes(width):
    units = width // LANES
    sizes = []
    left = units
    while left > 0:
        size = max(1, min(units // 4, (left + 1) // 2))
        sizes.append(size * LANES)
        left -= size
    return sizes


def shards(tokens, w_feat, short_filter, long_filter, doc_ids, grad_out):
    rows = tokens.shape[0]
    taps = long_filter.shape[1]
    short = short_filter.shape[2]
    channels = w_feat.shape[2]
    group = channels // long_filter.shape[0]
    tp = lax.axis_size("tp")
    reach = taps + EDGE

    sizes = chunk_sizes(channels)
    weights, start = [], 0
    for size in sizes:
        part = w_feat[:, :, start : start + size]
        weights.append(lax.all_gather(part, "fsdp", axis=1, tiled=True))
        start += size

    def extended(value):
        before = shifted(value[rows - reach :], "fsdp", 1)
        after = shifted(value[:reach], "fsdp", -1)
        return jnp.concatenate([before, value, after], axis=0)

    tokens_ext = gather_columns(extended(tokens), "tp")
    docs = extended(doc_ids + 1) - 1
    grad_ext = jnp.concatenate([grad_out, shifted(grad_out[:reach], "fsdp", -1)], axis=0)

    span = rows + 2 * taps + EDGE
    now = docs[EDGE : EDGE + span]
    back = sum((docs[EDGE - i : EDGE - i + span] == now).astype(jnp.int32) for i in range(1, short))
    back = jnp.broadcast_to(back[:, None], (span, LANES))
    ahead = sum(
        (docs[reach + i : reach + i + rows] == doc_ids).astype(jnp.int32) for i in range(1, short)
    )
    ahead = jnp.broadcast_to(ahead[:, None], (rows, LANES))

    near = rows + EDGE
    docs_pad = jnp.concatenate([docs, jnp.full((taps,), -1, docs.dtype)])

    def window_masks(lead):
        parts = []
        for at in range(0, near, taps):
            count = min(taps, near - at)
            own = docs_pad[reach + at : reach + at + count]
            cols = docs_pad[reach + at - lead : reach + at - lead + 2 * taps]
            parts.append(own[:, None] == cols[None, :])
        return jnp.concatenate(parts, axis=0).astype(jnp.bfloat16)

    m_fwd, m_bwd = window_masks(taps), window_masks(0)
    t_fwd, t_bwd = toeplitz(long_filter, False), toeplitz(long_filter, True)
    filters = jnp.pad(
        jnp.repeat(jnp.swapaxes(short_filter, 1, 2), group, axis=2), ((0, 0), (0, 8 - short), (0, 0))
    )

    wide = rows + taps + 2 * EDGE
    tokens_kv = tokens_ext[:wide]
    tokens_q = tokens_ext[taps:]
    mixed, partial, start = [], None, 0
    for size, w in zip(sizes, weights):
        u_q = jnp.dot(tokens_q, w[0], preferred_element_type=jnp.float32).astype(jnp.bfloat16)
        u_kv = jnp.einsum(
            "sd,jdc->jsc", tokens_kv, w[1:], preferred_element_type=jnp.float32
        ).astype(jnp.bfloat16)
        part, grad_u = convolve(
            rows, taps, short, start, u_q, u_kv, grad_ext, filters, t_fwd, t_bwd, m_fwd, m_bwd, back, ahead
        )
        mixed.append(part)
        term = jnp.einsum("jsc,jdc->sd", grad_u, w, preferred_element_type=jnp.float32)
        partial = term if partial is None else partial + term
        start += size
    mixed = jnp.concatenate(mixed, axis=1)

    partial = partial.astype(jnp.bfloat16)
    width = tokens.shape[1]
    here = lax.axis_index("tp")
    total = lax.dynamic_slice(partial, (0, here * width), (rows, width)).astype(jnp.float32)
    for step in range(1, tp):
        to = (here + step) % tp
        block = lax.dynamic_slice(partial, (0, to * width), (rows, width))
        total = total + rotated(block, "tp", step).astype(jnp.float32)
    return mixed, total.astype(jnp.bfloat16)


def solution(mesh):
    in_specs = (
        P("fsdp", "tp"),
        P(None, "fsdp", "tp"),
        P(None, "tp", None),
        P("tp", None),
        P("fsdp"),
        P("fsdp", "tp"),
    )
    out_specs = (P("fsdp", "tp"), P("fsdp", "tp"))
    return jax.shard_map(shards, mesh=mesh, in_specs=in_specs, out_specs=out_specs, check_vma=False)
```

```python
import functools

import jax
import jax.numpy as jnp
from jax import lax
from jax.experimental import pallas as pl
from jax.experimental.pallas import tpu as pltpu
from jax.sharding import PartitionSpec as P

LANES = 128
EDGE = 16


def shifted(value, axis, steps):
    count = lax.axis_size(axis)
    first, last = max(0, -steps), min(count, count - steps)
    return lax.ppermute(value, axis, [(at, at + steps) for at in range(first, last)])


def rotated(value, axis, steps):
    count = lax.axis_size(axis)
    return lax.ppermute(value, axis, [(at, (at + steps) % count) for at in range(count)])


def gather_columns(value, axis):
    count = lax.axis_size(axis)
    width = value.shape[1]
    here = lax.axis_index(axis)
    whole = jnp.zeros((value.shape[0], width * count), value.dtype)
    for step in range(count):
        block = value if step == 0 else rotated(value, axis, step)
        owner = (here - step) % count
        whole = lax.dynamic_update_slice(whole, block, (0, owner * width))
    return whole


def toeplitz(long_filter, anti_causal):
    taps = long_filter.shape[1]
    row = lax.broadcasted_iota(jnp.int32, (taps, 2 * taps), 0)
    column = lax.broadcasted_iota(jnp.int32, (taps, 2 * taps), 1)
    lag = column - row if anti_causal else row + taps - column
    tap = lax.broadcasted_iota(jnp.int32, (taps, taps, 2 * taps), 0)
    one_hot = (tap == lag[None]).astype(long_filter.dtype).reshape(taps, 2 * taps * taps)
    table = jnp.dot(long_filter, one_hot, preferred_element_type=jnp.float32)
    return table.astype(long_filter.dtype).reshape(long_filter.shape[0], taps, 2 * taps)


def conv_kernel(
    rows, taps, short,
    u_q, u_kv, grad, filters, t_fwd, t_bwd, m_fwd, m_bwd, back, ahead,
    mixed, grad_u,
    f32_u, conv, prod, glong, feat,
):
    near = rows + EDGE
    far = rows + taps + EDGE
    groups = t_fwd.shape[0]
    lane_group = lax.broadcasted_iota(jnp.int32, (1, LANES), 1) // (LANES // groups)

    def short_conv(role, source, first):
        f32_u[...] = source.astype(jnp.float32)
        total = filters[role, 0:1, :] * f32_u[pl.ds(EDGE, far), :]
        for i in range(1, short):
            term = filters[role, i : i + 1, :] * f32_u[pl.ds(EDGE - i, far), :]
            total = total + jnp.where(back[pl.ds(first, far), :] >= i, term, 0.0)
        return total

    conv[0] = short_conv(0, u_q[...], taps)
    conv[1] = short_conv(1, u_kv[0], 0)
    conv[2] = short_conv(2, u_kv[1], 0)
    pad = jnp.zeros((prod.shape[0] - far, LANES), prod.dtype)
    prod[pl.ds(0, far), :] = (conv[1] * conv[2]).astype(prod.dtype)
    prod[pl.ds(far, pad.shape[0]), :] = pad
    glong[pl.ds(0, far), :] = (grad[...].astype(jnp.float32) * conv[0]).astype(glong.dtype)
    glong[pl.ds(far, pad.shape[0]), :] = pad

    def long_conv(table, masks, source, start):
        count = min(taps, near - start)
        kernel = table[:, pl.ds(0, count), :] * masks[pl.ds(start, count), :][None]
        out = jnp.dot(
            kernel.reshape(groups * count, 2 * taps),
            source[pl.ds(start, 2 * taps), :],
            preferred_element_type=jnp.float32,
        ).reshape(groups, count, LANES)
        total = jnp.where(lane_group == 0, out[0], 0.0)
        for g in range(1, groups):
            total = jnp.where(lane_group == g, out[g], total)
        return total

    def rounded(value):
        return value.astype(jnp.bfloat16).astype(jnp.float32)

    for start in range(0, near, taps):
        count = min(taps, near - start)
        here = pl.ds(start, count)
        behind = pl.ds(start + taps, count)
        lc = long_conv(t_fwd, m_fwd, prod, start)
        gm = long_conv(t_bwd, m_bwd, glong, start)
        if start < rows:
            mixed[here, :] = (conv[0, here, :] * lc).astype(mixed.dtype)
        feat[0, here, :] = rounded(grad[here, :].astype(jnp.float32) * lc)
        feat[1, here, :] = rounded(gm * conv[2, behind, :])
        feat[2, here, :] = rounded(gm * conv[1, behind, :])
    for role in range(3):
        total = filters[role, 0:1, :] * feat[role, pl.ds(0, rows), :]
        for i in range(1, short):
            term = filters[role, i : i + 1, :] * feat[role, pl.ds(i, rows), :]
            total = total + jnp.where(ahead[...] >= i, term, 0.0)
        grad_u[role] = total.astype(grad_u.dtype)


def convolve(rows, taps, short, first, u_q, u_kv, grad, filters, t_fwd, t_bwd, m_fwd, m_bwd, back, ahead):
    width = u_q.shape[1]
    wide = u_q.shape[0]
    near, far = rows + EDGE, rows + taps + EDGE
    groups = t_fwd.shape[0] * LANES // grad.shape[1]
    first = first // LANES
    padded = rows + 2 * taps
    whole = lambda *shape: pl.BlockSpec(shape, lambda n: (0,) * len(shape))
    return pl.pallas_call(
        functools.partial(conv_kernel, rows, taps, short),
        grid=(width // LANES,),
        in_specs=[
            pl.BlockSpec((wide, LANES), lambda n: (0, n)),
            pl.BlockSpec((2, wide, LANES), lambda n: (0, 0, n)),
            pl.BlockSpec((far, LANES), lambda n: (0, n + first)),
            pl.BlockSpec((3, 8, LANES), lambda n: (0, 0, n + first)),
            pl.BlockSpec((groups, taps, 2 * taps), lambda n: (n + first, 0, 0)),
            pl.BlockSpec((groups, taps, 2 * taps), lambda n: (n + first, 0, 0)),
            whole(near, 2 * taps),
            whole(near, 2 * taps),
            whole(*back.shape),
            whole(*ahead.shape),
        ],
        out_specs=[
            pl.BlockSpec((rows, LANES), lambda n: (0, n)),
            pl.BlockSpec((3, rows, LANES), lambda n: (0, 0, n)),
        ],
        out_shape=[
            jax.ShapeDtypeStruct((rows, width), jnp.bfloat16),
            jax.ShapeDtypeStruct((3, rows, width), jnp.bfloat16),
        ],
        scratch_shapes=[
            pltpu.VMEM((wide, LANES), jnp.float32),
            pltpu.VMEM((3, far, LANES), jnp.float32),
            pltpu.VMEM((padded, LANES), jnp.bfloat16),
            pltpu.VMEM((padded, LANES), jnp.bfloat16),
            pltpu.VMEM((3, near, LANES), jnp.float32),
        ],
        compiler_params=pltpu.CompilerParams(vmem_limit_bytes=24 * 1024 * 1024),
        cost_estimate=pl.CostEstimate(
            flops=width * rows * taps * 64, bytes_accessed=width * rows * 40, transcendentals=0
        ),
    )(u_q, u_kv, grad, filters, t_fwd, t_bwd, m_fwd, m_bwd, back, ahead)


def chunk_sizes(width):
    last = max(1, width // LANES // 4) * LANES
    return [size for size in (width - last, last) if size > 0]


def shards(tokens, w_feat, short_filter, long_filter, doc_ids, grad_out):
    rows = tokens.shape[0]
    taps = long_filter.shape[1]
    short = short_filter.shape[2]
    channels = w_feat.shape[2]
    group = channels // long_filter.shape[0]
    tp = lax.axis_size("tp")
    reach = taps + EDGE

    sizes = chunk_sizes(channels)
    weights, start = [], 0
    for size in sizes:
        part = w_feat[:, :, start : start + size]
        weights.append(lax.all_gather(part, "fsdp", axis=1, tiled=True))
        start += size

    def extended(value):
        before = shifted(value[rows - reach :], "fsdp", 1)
        after = shifted(value[:reach], "fsdp", -1)
        return jnp.concatenate([before, value, after], axis=0)

    tokens_ext = gather_columns(extended(tokens), "tp")
    docs = extended(doc_ids + 1) - 1
    grad_ext = jnp.concatenate([grad_out, shifted(grad_out[:reach], "fsdp", -1)], axis=0)

    span = rows + 2 * taps + EDGE
    now = docs[EDGE : EDGE + span]
    back = sum((docs[EDGE - i : EDGE - i + span] == now).astype(jnp.int32) for i in range(1, short))
    back = jnp.broadcast_to(back[:, None], (span, LANES))
    ahead = sum(
        (docs[reach + i : reach + i + rows] == doc_ids).astype(jnp.int32) for i in range(1, short)
    )
    ahead = jnp.broadcast_to(ahead[:, None], (rows, LANES))

    near = rows + EDGE
    docs_pad = jnp.concatenate([docs, jnp.full((taps,), -1, docs.dtype)])

    def window_masks(lead):
        parts = []
        for at in range(0, near, taps):
            count = min(taps, near - at)
            own = docs_pad[reach + at : reach + at + count]
            cols = docs_pad[reach + at - lead : reach + at - lead + 2 * taps]
            parts.append(own[:, None] == cols[None, :])
        return jnp.concatenate(parts, axis=0).astype(jnp.bfloat16)

    m_fwd, m_bwd = window_masks(taps), window_masks(0)
    t_fwd, t_bwd = toeplitz(long_filter, False), toeplitz(long_filter, True)
    filters = jnp.pad(
        jnp.repeat(jnp.swapaxes(short_filter, 1, 2), group, axis=2), ((0, 0), (0, 8 - short), (0, 0))
    )

    wide = rows + taps + 2 * EDGE
    tokens_kv = tokens_ext[:wide]
    tokens_q = tokens_ext[taps:]
    mixed, partial, start = [], None, 0
    for size, w in zip(sizes, weights):
        if partial is not None:
            w, partial = lax.optimization_barrier((w, partial))
        u_q = jnp.dot(tokens_q, w[0], preferred_element_type=jnp.float32).astype(jnp.bfloat16)
        u_kv = jnp.einsum(
            "sd,jdc->jsc", tokens_kv, w[1:], preferred_element_type=jnp.float32
        ).astype(jnp.bfloat16)
        part, grad_u = convolve(
            rows, taps, short, start, u_q, u_kv, grad_ext, filters, t_fwd, t_bwd, m_fwd, m_bwd, back, ahead
        )
        mixed.append(part)
        term = jnp.einsum("jsc,jdc->sd", grad_u, w, preferred_element_type=jnp.float32)
        partial = term if partial is None else partial + term
        start += size
    mixed = jnp.concatenate(mixed, axis=1)

    partial = partial.astype(jnp.bfloat16)
    width = tokens.shape[1]
    here = lax.axis_index("tp")
    total = lax.dynamic_slice(partial, (0, here * width), (rows, width)).astype(jnp.float32)
    for step in range(1, tp):
        to = (here + step) % tp
        block = lax.dynamic_slice(partial, (0, to * width), (rows, width))
        total = total + rotated(block, "tp", step).astype(jnp.float32)
    return mixed, total.astype(jnp.bfloat16)


def solution(mesh):
    in_specs = (
        P("fsdp", "tp"),
        P(None, "fsdp", "tp"),
        P(None, "tp", None),
        P("tp", None),
        P("fsdp"),
        P("fsdp", "tp"),
    )
    out_specs = (P("fsdp", "tp"), P("fsdp", "tp"))
    return jax.shard_map(shards, mesh=mesh, in_specs=in_specs, out_specs=out_specs, check_vma=False)
```

```python
import functools

import jax
import jax.numpy as jnp
from jax import lax
from jax.experimental import pallas as pl
from jax.experimental.pallas import tpu as pltpu
from jax.sharding import PartitionSpec as P

LANES = 128
EDGE = 16


def shifted(value, axis, steps):
    count = lax.axis_size(axis)
    first, last = max(0, -steps), min(count, count - steps)
    return lax.ppermute(value, axis, [(at, at + steps) for at in range(first, last)])


def rotated(value, axis, steps):
    count = lax.axis_size(axis)
    return lax.ppermute(value, axis, [(at, (at + steps) % count) for at in range(count)])


def gather_columns(value, axis):
    count = lax.axis_size(axis)
    width = value.shape[1]
    here = lax.axis_index(axis)
    whole = jnp.zeros((value.shape[0], width * count), value.dtype)
    for step in range(count):
        block = value if step == 0 else rotated(value, axis, step)
        owner = (here - step) % count
        whole = lax.dynamic_update_slice(whole, block, (0, owner * width))
    return whole


def toeplitz(long_filter, anti_causal):
    taps = long_filter.shape[1]
    row = lax.broadcasted_iota(jnp.int32, (taps, 2 * taps), 0)
    column = lax.broadcasted_iota(jnp.int32, (taps, 2 * taps), 1)
    lag = column - row if anti_causal else row + taps - column
    tap = lax.broadcasted_iota(jnp.int32, (taps, taps, 2 * taps), 0)
    one_hot = (tap == lag[None]).astype(long_filter.dtype).reshape(taps, 2 * taps * taps)
    table = jnp.dot(long_filter, one_hot, preferred_element_type=jnp.float32)
    return table.astype(long_filter.dtype).reshape(long_filter.shape[0], taps, 2 * taps)


def conv_kernel(
    rows, taps, short,
    u_q, u_kv, grad, filters, t_fwd, t_bwd, m_fwd, m_bwd, back, ahead,
    mixed, grad_u,
    f32_u, conv, prod, glong, feat,
):
    near = rows + EDGE
    far = rows + taps + EDGE
    groups = t_fwd.shape[0]
    lane_group = lax.broadcasted_iota(jnp.int32, (1, LANES), 1) // (LANES // groups)

    def short_conv(role, source, first):
        f32_u[...] = source.astype(jnp.float32)
        total = filters[role, 0:1, :] * f32_u[pl.ds(EDGE, far), :]
        for i in range(1, short):
            term = filters[role, i : i + 1, :] * f32_u[pl.ds(EDGE - i, far), :]
            total = total + jnp.where(back[pl.ds(first, far), :] >= i, term, 0.0)
        return total

    conv[0] = short_conv(0, u_q[...], taps)
    conv[1] = short_conv(1, u_kv[0], 0)
    conv[2] = short_conv(2, u_kv[1], 0)
    pad = jnp.zeros((prod.shape[0] - far, LANES), prod.dtype)
    prod[pl.ds(0, far), :] = (conv[1] * conv[2]).astype(prod.dtype)
    prod[pl.ds(far, pad.shape[0]), :] = pad
    glong[pl.ds(0, far), :] = (grad[...].astype(jnp.float32) * conv[0]).astype(glong.dtype)
    glong[pl.ds(far, pad.shape[0]), :] = pad

    def long_conv(table, masks, source, start):
        count = min(taps, near - start)
        kernel = table[:, pl.ds(0, count), :] * masks[pl.ds(start, count), :][None]
        out = jnp.dot(
            kernel.reshape(groups * count, 2 * taps),
            source[pl.ds(start, 2 * taps), :],
            preferred_element_type=jnp.float32,
        ).reshape(groups, count, LANES)
        total = jnp.where(lane_group == 0, out[0], 0.0)
        for g in range(1, groups):
            total = jnp.where(lane_group == g, out[g], total)
        return total

    def rounded(value):
        return value.astype(jnp.bfloat16).astype(jnp.float32)

    for start in range(0, near, taps):
        count = min(taps, near - start)
        here = pl.ds(start, count)
        behind = pl.ds(start + taps, count)
        lc = long_conv(t_fwd, m_fwd, prod, start)
        gm = long_conv(t_bwd, m_bwd, glong, start)
        if start < rows:
            mixed[here, :] = (conv[0, here, :] * lc).astype(mixed.dtype)
        feat[0, here, :] = rounded(grad[here, :].astype(jnp.float32) * lc)
        feat[1, here, :] = rounded(gm * conv[2, behind, :])
        feat[2, here, :] = rounded(gm * conv[1, behind, :])
    for role in range(3):
        total = filters[role, 0:1, :] * feat[role, pl.ds(0, rows), :]
        for i in range(1, short):
            term = filters[role, i : i + 1, :] * feat[role, pl.ds(i, rows), :]
            total = total + jnp.where(ahead[...] >= i, term, 0.0)
        grad_u[role] = total.astype(grad_u.dtype)


def convolve(rows, taps, short, first, u_q, u_kv, grad, filters, t_fwd, t_bwd, m_fwd, m_bwd, back, ahead):
    width = u_q.shape[1]
    wide = u_q.shape[0]
    near, far = rows + EDGE, rows + taps + EDGE
    groups = t_fwd.shape[0] * LANES // grad.shape[1]
    first = first // LANES
    padded = rows + 2 * taps
    whole = lambda *shape: pl.BlockSpec(shape, lambda n: (0,) * len(shape))
    return pl.pallas_call(
        functools.partial(conv_kernel, rows, taps, short),
        grid=(width // LANES,),
        in_specs=[
            pl.BlockSpec((wide, LANES), lambda n: (0, n)),
            pl.BlockSpec((2, wide, LANES), lambda n: (0, 0, n)),
            pl.BlockSpec((far, LANES), lambda n: (0, n + first)),
            pl.BlockSpec((3, 8, LANES), lambda n: (0, 0, n + first)),
            pl.BlockSpec((groups, taps, 2 * taps), lambda n: (n + first, 0, 0)),
            pl.BlockSpec((groups, taps, 2 * taps), lambda n: (n + first, 0, 0)),
            whole(near, 2 * taps),
            whole(near, 2 * taps),
            whole(*back.shape),
            whole(*ahead.shape),
        ],
        out_specs=[
            pl.BlockSpec((rows, LANES), lambda n: (0, n)),
            pl.BlockSpec((3, rows, LANES), lambda n: (0, 0, n)),
        ],
        out_shape=[
            jax.ShapeDtypeStruct((rows, width), jnp.bfloat16),
            jax.ShapeDtypeStruct((3, rows, width), jnp.bfloat16),
        ],
        scratch_shapes=[
            pltpu.VMEM((wide, LANES), jnp.float32),
            pltpu.VMEM((3, far, LANES), jnp.float32),
            pltpu.VMEM((padded, LANES), jnp.bfloat16),
            pltpu.VMEM((padded, LANES), jnp.bfloat16),
            pltpu.VMEM((3, near, LANES), jnp.float32),
        ],
        compiler_params=pltpu.CompilerParams(vmem_limit_bytes=57 * 1024 * 1024),
        cost_estimate=pl.CostEstimate(
            flops=width * rows * taps * 64, bytes_accessed=width * rows * 40, transcendentals=0
        ),
    )(u_q, u_kv, grad, filters, t_fwd, t_bwd, m_fwd, m_bwd, back, ahead)


def chunk_sizes(width):
    last = max(1, width // LANES * 3 // 16) * LANES
    return [size for size in (width - last, last) if size > 0]


def shards(tokens, w_feat, short_filter, long_filter, doc_ids, grad_out):
    rows = tokens.shape[0]
    taps = long_filter.shape[1]
    short = short_filter.shape[2]
    channels = w_feat.shape[2]
    group = channels // long_filter.shape[0]
    tp = lax.axis_size("tp")
    reach = taps + EDGE

    sizes = chunk_sizes(channels)
    weights, start = [], 0
    for size in sizes:
        part = w_feat[:, :, start : start + size]
        weights.append(lax.all_gather(part, "fsdp", axis=1, tiled=True))
        start += size

    def extended(value):
        before = shifted(value[rows - reach :], "fsdp", 1)
        after = shifted(value[:reach], "fsdp", -1)
        return jnp.concatenate([before, value, after], axis=0)

    tokens_ext = gather_columns(extended(tokens), "tp")
    docs = extended(doc_ids + 1) - 1
    grad_ext = jnp.concatenate([grad_out, shifted(grad_out[:reach], "fsdp", -1)], axis=0)

    span = rows + 2 * taps + EDGE
    now = docs[EDGE : EDGE + span]
    back = sum((docs[EDGE - i : EDGE - i + span] == now).astype(jnp.int32) for i in range(1, short))
    back = jnp.broadcast_to(back[:, None], (span, LANES))
    ahead = sum(
        (docs[reach + i : reach + i + rows] == doc_ids).astype(jnp.int32) for i in range(1, short)
    )
    ahead = jnp.broadcast_to(ahead[:, None], (rows, LANES))

    near = rows + EDGE
    docs_pad = jnp.concatenate([docs, jnp.full((taps,), -1, docs.dtype)])

    def window_masks(lead):
        parts = []
        for at in range(0, near, taps):
            count = min(taps, near - at)
            own = docs_pad[reach + at : reach + at + count]
            cols = docs_pad[reach + at - lead : reach + at - lead + 2 * taps]
            parts.append(own[:, None] == cols[None, :])
        return jnp.concatenate(parts, axis=0).astype(jnp.bfloat16)

    m_fwd, m_bwd = window_masks(taps), window_masks(0)
    t_fwd, t_bwd = toeplitz(long_filter, False), toeplitz(long_filter, True)
    filters = jnp.pad(
        jnp.repeat(jnp.swapaxes(short_filter, 1, 2), group, axis=2), ((0, 0), (0, 8 - short), (0, 0))
    )

    wide = rows + taps + 2 * EDGE
    tokens_kv = tokens_ext[:wide]
    tokens_q = tokens_ext[taps:]
    mixed, partial, start = [], None, 0
    for size, w in zip(sizes, weights):
        if partial is not None:
            w, partial = lax.optimization_barrier((w, partial))
        u_q = jnp.dot(tokens_q, w[0], preferred_element_type=jnp.float32).astype(jnp.bfloat16)
        u_kv = jnp.einsum(
            "sd,jdc->jsc", tokens_kv, w[1:], preferred_element_type=jnp.float32
        ).astype(jnp.bfloat16)
        part, grad_u = convolve(
            rows, taps, short, start, u_q, u_kv, grad_ext, filters, t_fwd, t_bwd, m_fwd, m_bwd, back, ahead
        )
        mixed.append(part)
        term = jnp.einsum("jsc,jdc->sd", grad_u, w, preferred_element_type=jnp.float32)
        partial = term if partial is None else partial + term
        start += size
    mixed = jnp.concatenate(mixed, axis=1)

    partial = partial.astype(jnp.bfloat16)
    width = tokens.shape[1]
    here = lax.axis_index("tp")
    total = lax.dynamic_slice(partial, (0, here * width), (rows, width)).astype(jnp.float32)
    for step in range(1, tp):
        to = (here + step) % tp
        block = lax.dynamic_slice(partial, (0, to * width), (rows, width))
        total = total + rotated(block, "tp", step).astype(jnp.float32)
    return mixed, total.astype(jnp.bfloat16)


def solution(mesh):
    in_specs = (
        P("fsdp", "tp"),
        P(None, "fsdp", "tp"),
        P(None, "tp", None),
        P("tp", None),
        P("fsdp"),
        P("fsdp", "tp"),
    )
    out_specs = (P("fsdp", "tp"), P("fsdp", "tp"))
    return jax.shard_map(shards, mesh=mesh, in_specs=in_specs, out_specs=out_specs, check_vma=False)
```

```python
import functools

import jax
import jax.numpy as jnp
from jax import lax
from jax.experimental import pallas as pl
from jax.experimental.pallas import tpu as pltpu
from jax.sharding import PartitionSpec as P

LANES = 128
EDGE = 16


def shifted(value, axis, steps):
    count = lax.axis_size(axis)
    first, last = max(0, -steps), min(count, count - steps)
    return lax.ppermute(value, axis, [(at, at + steps) for at in range(first, last)])


def rotated(value, axis, steps):
    count = lax.axis_size(axis)
    return lax.ppermute(value, axis, [(at, (at + steps) % count) for at in range(count)])


def gather_columns(value, axis):
    count = lax.axis_size(axis)
    width = value.shape[1]
    here = lax.axis_index(axis)
    whole = jnp.zeros((value.shape[0], width * count), value.dtype)
    for step in range(count):
        block = value if step == 0 else rotated(value, axis, step)
        owner = (here - step) % count
        whole = lax.dynamic_update_slice(whole, block, (0, owner * width))
    return whole


def toeplitz(long_filter, anti_causal):
    taps = long_filter.shape[1]
    row = lax.broadcasted_iota(jnp.int32, (taps, 2 * taps), 0)
    column = lax.broadcasted_iota(jnp.int32, (taps, 2 * taps), 1)
    lag = column - row if anti_causal else row + taps - column
    tap = lax.broadcasted_iota(jnp.int32, (taps, taps, 2 * taps), 0)
    one_hot = (tap == lag[None]).astype(long_filter.dtype).reshape(taps, 2 * taps * taps)
    table = jnp.dot(long_filter, one_hot, preferred_element_type=jnp.float32)
    return table.astype(long_filter.dtype).reshape(long_filter.shape[0], taps, 2 * taps)


def conv_kernel(
    rows, taps, short,
    u_q, u_kv, grad, filters, t_fwd, t_bwd, m_fwd, m_bwd, back, ahead,
    mixed, grad_u,
    f32_u, conv, prod, glong, feat,
):
    near = rows + EDGE
    far = rows + taps + EDGE
    groups = t_fwd.shape[0]
    lane_group = lax.broadcasted_iota(jnp.int32, (1, LANES), 1) // (LANES // groups)

    def short_conv(role, source, first):
        f32_u[...] = source.astype(jnp.float32)
        total = filters[role, 0:1, :] * f32_u[pl.ds(EDGE, far), :]
        for i in range(1, short):
            term = filters[role, i : i + 1, :] * f32_u[pl.ds(EDGE - i, far), :]
            total = total + jnp.where(back[pl.ds(first, far), :] >= i, term, 0.0)
        return total

    conv[0] = short_conv(0, u_q[...], taps)
    conv[1] = short_conv(1, u_kv[0], 0)
    conv[2] = short_conv(2, u_kv[1], 0)
    pad = jnp.zeros((prod.shape[0] - far, LANES), prod.dtype)
    prod[pl.ds(0, far), :] = (conv[1] * conv[2]).astype(prod.dtype)
    prod[pl.ds(far, pad.shape[0]), :] = pad
    glong[pl.ds(0, far), :] = (grad[...].astype(jnp.float32) * conv[0]).astype(glong.dtype)
    glong[pl.ds(far, pad.shape[0]), :] = pad

    def long_conv(table, masks, source, start):
        count = min(taps, near - start)
        kernel = table[:, pl.ds(0, count), :] * masks[pl.ds(start, count), :][None]
        out = jnp.dot(
            kernel.reshape(groups * count, 2 * taps),
            source[pl.ds(start, 2 * taps), :],
            preferred_element_type=jnp.float32,
        ).reshape(groups, count, LANES)
        total = jnp.where(lane_group == 0, out[0], 0.0)
        for g in range(1, groups):
            total = jnp.where(lane_group == g, out[g], total)
        return total

    def rounded(value):
        return value.astype(jnp.bfloat16).astype(jnp.float32)

    for start in range(0, near, taps):
        count = min(taps, near - start)
        here = pl.ds(start, count)
        behind = pl.ds(start + taps, count)
        lc = long_conv(t_fwd, m_fwd, prod, start)
        gm = long_conv(t_bwd, m_bwd, glong, start)
        if start < rows:
            mixed[here, :] = (conv[0, here, :] * lc).astype(mixed.dtype)
        feat[0, here, :] = rounded(grad[here, :].astype(jnp.float32) * lc)
        feat[1, here, :] = rounded(gm * conv[2, behind, :])
        feat[2, here, :] = rounded(gm * conv[1, behind, :])
    for role in range(3):
        total = filters[role, 0:1, :] * feat[role, pl.ds(0, rows), :]
        for i in range(1, short):
            term = filters[role, i : i + 1, :] * feat[role, pl.ds(i, rows), :]
            total = total + jnp.where(ahead[...] >= i, term, 0.0)
        grad_u[role] = total.astype(grad_u.dtype)


def convolve(rows, taps, short, first, u_q, u_kv, grad, filters, t_fwd, t_bwd, m_fwd, m_bwd, back, ahead):
    width = u_q.shape[1]
    wide = u_q.shape[0]
    near, far = rows + EDGE, rows + taps + EDGE
    groups = t_fwd.shape[0] * LANES // grad.shape[1]
    first = first // LANES
    padded = rows + 2 * taps
    whole = lambda *shape: pl.BlockSpec(shape, lambda n: (0,) * len(shape))
    return pl.pallas_call(
        functools.partial(conv_kernel, rows, taps, short),
        grid=(width // LANES,),
        in_specs=[
            pl.BlockSpec((wide, LANES), lambda n: (0, n)),
            pl.BlockSpec((2, wide, LANES), lambda n: (0, 0, n)),
            pl.BlockSpec((far, LANES), lambda n: (0, n + first)),
            pl.BlockSpec((3, 8, LANES), lambda n: (0, 0, n + first)),
            pl.BlockSpec((groups, taps, 2 * taps), lambda n: (n + first, 0, 0)),
            pl.BlockSpec((groups, taps, 2 * taps), lambda n: (n + first, 0, 0)),
            whole(near, 2 * taps),
            whole(near, 2 * taps),
            whole(*back.shape),
            whole(*ahead.shape),
        ],
        out_specs=[
            pl.BlockSpec((rows, LANES), lambda n: (0, n)),
            pl.BlockSpec((3, rows, LANES), lambda n: (0, 0, n)),
        ],
        out_shape=[
            jax.ShapeDtypeStruct((rows, width), jnp.bfloat16),
            jax.ShapeDtypeStruct((3, rows, width), jnp.bfloat16),
        ],
        scratch_shapes=[
            pltpu.VMEM((wide, LANES), jnp.float32),
            pltpu.VMEM((3, far, LANES), jnp.float32),
            pltpu.VMEM((padded, LANES), jnp.bfloat16),
            pltpu.VMEM((padded, LANES), jnp.bfloat16),
            pltpu.VMEM((3, near, LANES), jnp.float32),
        ],
        compiler_params=pltpu.CompilerParams(vmem_limit_bytes=57 * 1024 * 1024),
        cost_estimate=pl.CostEstimate(
            flops=width * rows * taps * 64, bytes_accessed=width * rows * 40, transcendentals=0
        ),
    )(u_q, u_kv, grad, filters, t_fwd, t_bwd, m_fwd, m_bwd, back, ahead)


def chunk_sizes(width):
    last = max(1, width // LANES * 3 // 16) * LANES
    return [size for size in (width - last, last) if size > 0]


def backward(grad_u, w):
    return jnp.einsum("jsc,jdc->sd", grad_u, w, preferred_element_type=jnp.float32)


def shards(tokens, w_feat, short_filter, long_filter, doc_ids, grad_out):
    rows = tokens.shape[0]
    taps = long_filter.shape[1]
    short = short_filter.shape[2]
    channels = w_feat.shape[2]
    group = channels // long_filter.shape[0]
    tp = lax.axis_size("tp")
    reach = taps + EDGE

    sizes = chunk_sizes(channels)
    weights, start = [], 0
    for size in sizes:
        part = w_feat[:, :, start : start + size]
        weights.append(lax.all_gather(part, "fsdp", axis=1, tiled=True))
        start += size

    def extended(value):
        before = shifted(value[rows - reach :], "fsdp", 1)
        after = shifted(value[:reach], "fsdp", -1)
        return jnp.concatenate([before, value, after], axis=0)

    tokens_ext = gather_columns(extended(tokens), "tp")
    docs = extended(doc_ids + 1) - 1
    grad_ext = jnp.concatenate([grad_out, shifted(grad_out[:reach], "fsdp", -1)], axis=0)

    span = rows + 2 * taps + EDGE
    now = docs[EDGE : EDGE + span]
    back = sum((docs[EDGE - i : EDGE - i + span] == now).astype(jnp.int32) for i in range(1, short))
    back = jnp.broadcast_to(back[:, None], (span, LANES))
    ahead = sum(
        (docs[reach + i : reach + i + rows] == doc_ids).astype(jnp.int32) for i in range(1, short)
    )
    ahead = jnp.broadcast_to(ahead[:, None], (rows, LANES))

    near = rows + EDGE
    docs_pad = jnp.concatenate([docs, jnp.full((taps,), -1, docs.dtype)])

    def window_masks(lead):
        parts = []
        for at in range(0, near, taps):
            count = min(taps, near - at)
            own = docs_pad[reach + at : reach + at + count]
            cols = docs_pad[reach + at - lead : reach + at - lead + 2 * taps]
            parts.append(own[:, None] == cols[None, :])
        return jnp.concatenate(parts, axis=0).astype(jnp.bfloat16)

    m_fwd, m_bwd = window_masks(taps), window_masks(0)
    t_fwd, t_bwd = toeplitz(long_filter, False), toeplitz(long_filter, True)
    filters = jnp.pad(
        jnp.repeat(jnp.swapaxes(short_filter, 1, 2), group, axis=2), ((0, 0), (0, 8 - short), (0, 0))
    )

    wide = rows + taps + 2 * EDGE
    tokens_kv = tokens_ext[:wide]
    tokens_q = tokens_ext[taps:]
    mixed, partial, start = [], None, 0
    for size, w in zip(sizes, weights):
        if partial is not None:
            w, partial = lax.optimization_barrier((w, partial))
        u_q = jnp.dot(tokens_q, w[0], preferred_element_type=jnp.float32).astype(jnp.bfloat16)
        u_kv = jnp.einsum(
            "sd,jdc->jsc", tokens_kv, w[1:], preferred_element_type=jnp.float32
        ).astype(jnp.bfloat16)
        part, grad_u = convolve(
            rows, taps, short, start, u_q, u_kv, grad_ext, filters, t_fwd, t_bwd, m_fwd, m_bwd, back, ahead
        )
        mixed.append(part)
        if start + size < channels:
            term = backward(grad_u, w)
            partial = term if partial is None else partial + term
        start += size
    mixed = jnp.concatenate(mixed, axis=1)

    width = tokens.shape[1]
    here = lax.axis_index("tp")
    half = rows // 2
    outs = []
    for at in (0, half):
        term = backward(grad_u[:, at : at + half], w)
        if partial is not None:
            term = partial[at : at + half] + term
        term = term.astype(jnp.bfloat16)
        total = lax.dynamic_slice(term, (0, here * width), (half, width)).astype(jnp.float32)
        for step in range(1, tp):
            to = (here + step) % tp
            block = lax.dynamic_slice(term, (0, to * width), (half, width))
            total = total + rotated(block, "tp", step).astype(jnp.float32)
        outs.append(total.astype(jnp.bfloat16))
    return mixed, jnp.concatenate(outs, axis=0)


def solution(mesh):
    in_specs = (
        P("fsdp", "tp"),
        P(None, "fsdp", "tp"),
        P(None, "tp", None),
        P("tp", None),
        P("fsdp"),
        P("fsdp", "tp"),
    )
    out_specs = (P("fsdp", "tp"), P("fsdp", "tp"))
    return jax.shard_map(shards, mesh=mesh, in_specs=in_specs, out_specs=out_specs, check_vma=False)
```
